32 devices in a mesh: grp: 2 (over x), wide: 16 (over z, y, core).
Axes of the slice: x: 2, y: 2, z: 4, core: 2. Of those that a mesh axis runs over, the one named last changes fastest.
Arguments:
- voltages: bfloat16 [2048, 131, 2048], P(('grp', 'wide')), parts along dimension 0, may hold values from -6 to 6
- filter_taps: bfloat16 [4, 2048], replicated, may hold values from -3 to 3
- input_gain: float32 [2048], P(('grp', 'wide')), parts along dimension 0, may hold values from 0.5 to 11, as said below
- input_flags: int32 [2048], P(('grp', 'wide')), parts along dimension 0, may hold values 0 or 1
- kept_channels: int32 [256], replicated, may hold values from 0 to 1023, as said below
- tile_order: int32 [10], replicated, may hold values from 0 to 9, each once
Outputs:
- visibilities: bfloat16 [512, 10, 2, 256, 256], P(('grp', 'wide')), parts along dimension 0
The draws below stay inside these ranges and needn't reach their ends.
There are 2 independent parts, one for each index of `grp`. The reference program is written for one: setup_inputs(seed, part) draws one part's arguments, and reference() takes and returns one part's arrays. A program takes and returns all parts, laid end to end along the dimension named above; an argument that names none is the same for every part. Nothing has to cross between parts.
Inputs may be any that keep to these rules, and one draw needn't show every extreme that they name: `kept_channels`: the 256 channel numbers are distinct; channels 0 and 1023 are always among them. `tile_order`: each tile number appears once. `input_gain`: gains are positive.
All inputs are finite; a program needn't handle non-finite values. No bound on the sum of `input_flags` on one device may be relied on, other than what follows from the above.
Results may differ from the reference program's by a relative error of at most 0.007.
Values may be sent and summed in bfloat16 or wider, within the bound.
A program may use at most 448 MiB of HBM per device.

```python
import math
import jax
import jax.numpy as jnp
from jax import lax

INPUTS = 1024
CHANNELS = 1024
SAMPLES = 2048
KEPT = 256
TAPS = 4
BLK = 256
TILES = 10
FRAMES = 128


def draw_input_gain(key, part):
    position = jnp.arange(INPUTS, dtype=jnp.float32) / INPUTS
    spread = jax.random.uniform(key, (INPUTS,), jnp.float32, 0.6, 1.4)
    return jnp.power(jnp.float32(3.0), position) * spread


def draw_kept_channels(key, part):
    inner = 1 + jax.random.permutation(key, CHANNELS - 2)[:KEPT - 2]
    whole = jnp.concatenate([jnp.zeros((1,), jnp.int32), inner.astype(jnp.int32), jnp.full((1,), CHANNELS - 1, jnp.int32)])
    shuffle = jax.random.permutation(jax.random.fold_in(key, 7), KEPT)
    return whole[shuffle].astype(jnp.int32)


def with_ends(drawn, key, low, top_value):
    longest = drawn.shape.index(max(drawn.shape))
    spots = []
    for shift in (0, 1):
        where = [jax.random.randint(jax.random.fold_in(key, axis), (), 0, length) for axis, length in enumerate(drawn.shape)]
        where[longest] = (where[longest] + shift) % drawn.shape[longest]
        spots.append(tuple(where))
    return drawn.at[spots[0]].set(low).at[spots[1]].set(top_value)


def block_levels(rng, extent, shards, smallest, top_value):
    level, own = 1.0, jax.random.fold_in(rng, 6)
    for dim, shards_of in shards:
        draws = jnp.exp(jax.random.uniform(jax.random.fold_in(own, dim), (shards_of,), jnp.float32, smallest / len(shards), top_value / len(shards)))
        level = level * jnp.repeat(draws, extent[dim] // shards_of).reshape([-1 if axis == dim else 1 for axis in range(len(extent))])
    return level


def gaussian(rng, dims, scale, reach, pieces=(), kind=jnp.bfloat16):
    level = block_levels(rng, dims, pieces, -0.22, 0.18) if pieces else 1.0
    entries = jax.random.normal(rng, dims, jnp.float32) * scale * level
    return jnp.minimum(jnp.maximum(entries, -reach), reach).astype(kind)


def setup_inputs(seed: int = 0, part: int = 0) -> dict:
    streams_of = jax.random.split(jax.random.key(seed), 7)
    part_keys = jax.random.split(jax.random.fold_in(streams_of[6], part), 7)
    voltages = gaussian(part_keys[0], (INPUTS, FRAMES + TAPS - 1, SAMPLES), 1.0, 6.0, ((0, 16),))
    filter_taps = gaussian(streams_of[1], (TAPS, SAMPLES), 0.5, 3.0)
    input_gain = draw_input_gain(jax.random.fold_in(jax.random.fold_in(streams_of[6], part), 71), part)
    input_flags = with_ends((jax.random.randint(part_keys[3], (INPUTS,), 0, 8) < 7).astype(jnp.int32), jax.random.fold_in(part_keys[3], 1), 0, 1)
    kept_channels = draw_kept_channels(jax.random.fold_in(streams_of[6], 71), part)
    tile_order = jax.random.permutation(streams_of[5], TILES).astype(jnp.int32)
    return dict(voltages=voltages, filter_taps=filter_taps, input_gain=input_gain, input_flags=input_flags, kept_channels=kept_channels, tile_order=tile_order)


eps_power = 1e-06

def tile_tables(blocks):
    row_list = []
    col_list = []
    for row_block in range(blocks):
        for col_block in range(row_block, blocks):
            row_list.append(row_block)
            col_list.append(col_block)
    return (row_list, col_list)

def dft_table(kept_channels, samples):
    sample_index = jnp.arange(samples, dtype=jnp.int32)
    product = sample_index[:, None] * kept_channels.astype(jnp.int32)[None, :] % samples
    phase = product.astype(jnp.float32) * jnp.float32(2.0 * math.pi / samples)
    factor = jnp.float32(1.0 / math.sqrt(samples / 2))
    return jnp.concatenate([jnp.cos(phase) * factor, -jnp.sin(phase) * factor], axis=1).astype(jnp.bfloat16)

def reference(voltages, filter_taps, input_gain, input_flags, kept_channels, tile_order):
    table = dft_table(kept_channels, SAMPLES)
    blocks = INPUTS // BLK
    volt_blocks = voltages.reshape(blocks, BLK, FRAMES + TAPS - 1, SAMPLES)
    gain_blocks = input_gain.reshape(blocks, BLK)
    flag_blocks = input_flags.astype(jnp.float32).reshape(blocks, BLK)

    def transform(piece):
        volt, gains, flags = piece
        filtered = jnp.zeros((BLK, FRAMES, SAMPLES), jnp.float32)
        for tap_index in range(TAPS):
            filtered = filtered + volt[:, tap_index:tap_index + FRAMES, :].astype(jnp.float32) * filter_taps[tap_index].astype(jnp.float32)
        filtered = (filtered * gains[:, None, None]).astype(jnp.bfloat16)
        spectra = jnp.dot(filtered.reshape(BLK * FRAMES, SAMPLES), table, preferred_element_type=jnp.float32)
        return spectra.reshape(BLK, FRAMES, 2 * KEPT) * flags[:, None, None]
    spectra = lax.map(transform, (volt_blocks, gain_blocks, flag_blocks)).reshape(INPUTS, FRAMES, 2 * KEPT)
    squares = spectra[:, :, :KEPT] * spectra[:, :, :KEPT] + spectra[:, :, KEPT:] * spectra[:, :, KEPT:]
    power = lax.optimization_barrier(jnp.sum(squares, axis=(0, 1))) / jnp.float32(INPUTS * FRAMES) + jnp.float32(eps_power)
    scale = lax.rsqrt(power)
    equalized = (spectra * jnp.concatenate([scale, scale])[None, None, :]).astype(jnp.bfloat16)
    turned = equalized.reshape(INPUTS, FRAMES, 2, KEPT).transpose(3, 2, 1, 0)
    row_list, col_list = tile_tables(blocks)

    def correlate(channel):
        real_part = channel[0]
        imag_part = channel[1]
        stacked = jnp.concatenate([real_part, imag_part], axis=0)
        rotated = jnp.concatenate([imag_part, -real_part], axis=0)
        real_full = jnp.dot(stacked.T, stacked, preferred_element_type=jnp.float32)
        imag_full = jnp.dot(rotated.T, stacked, preferred_element_type=jnp.float32)
        tile_list = []
        for row_block, col_block in zip(row_list, col_list):
            real_tile = real_full[row_block * BLK:(row_block + 1) * BLK, col_block * BLK:(col_block + 1) * BLK]
            imag_tile = imag_full[row_block * BLK:(row_block + 1) * BLK, col_block * BLK:(col_block + 1) * BLK]
            tile_list.append(jnp.stack([real_tile, imag_tile]))
        every = jnp.stack(tile_list) * jnp.float32(1.0 / FRAMES)
        return jnp.take(every, tile_order.astype(jnp.int32), axis=0).astype(jnp.bfloat16)
    return lax.map(correlate, turned)
```

```python
import functools
import math

import jax
import jax.numpy as jnp
import numpy as np
from jax import lax
from jax.experimental import pallas as pl
from jax.experimental.pallas import tpu as pltpu
from jax.sharding import PartitionSpec as P

BLK = 256


eps_power = 1e-06


def tile_tables(blocks):
    row_list = []
    col_list = []
    for row_block in range(blocks):
        for col_block in range(row_block, blocks):
            row_list.append(row_block)
            col_list.append(col_block)
    return (np.array(row_list, np.int32), np.array(col_list, np.int32))


def dft_table(kept_channels, samples):
    sample_index = jnp.arange(samples, dtype=jnp.int32)
    product = sample_index[:, None] * kept_channels[None, :] % samples
    phase = product.astype(jnp.float32) * jnp.float32(2.0 * math.pi / samples)
    factor = jnp.float32(1.0 / math.sqrt(samples / 2))
    return jnp.concatenate([jnp.cos(phase) * factor, -jnp.sin(phase) * factor], axis=1).astype(
        jnp.bfloat16
    )


def tile_corner(tile_order, slot_index, corner_table):
    picked = tile_order[slot_index] == jnp.arange(corner_table.shape[0], dtype=jnp.int32)
    return jnp.sum(jnp.where(picked, jnp.asarray(corner_table), 0)).astype(jnp.int32)


def visibility_terms(turned, tile_order, block_size):
    real_part = turned[:, 0]
    imag_part = turned[:, 1]
    stacked = jnp.concatenate([real_part, imag_part], axis=1)
    rotated = jnp.concatenate([imag_part, -real_part], axis=1)
    local_channels = turned.shape[0]
    row_table, col_table = tile_tables(turned.shape[3] // block_size)
    tile_list = []
    real_full = jnp.einsum("cfi,cfj->cij", stacked, stacked, preferred_element_type=jnp.float32)
    imag_full = jnp.einsum("cfi,cfj->cij", rotated, stacked, preferred_element_type=jnp.float32)
    for slot_index in range(row_table.shape[0]):
        row_start = tile_corner(tile_order, slot_index, row_table) * block_size
        col_start = tile_corner(tile_order, slot_index, col_table) * block_size
        zero_start = jnp.zeros((), jnp.int32)
        real_tile = lax.dynamic_slice(
            real_full, (zero_start, row_start, col_start), (local_channels, block_size, block_size)
        )
        imag_tile = lax.dynamic_slice(
            imag_full, (zero_start, row_start, col_start), (local_channels, block_size, block_size)
        )
        tile_list.append(jnp.stack([real_tile, imag_tile], axis=1))
    return jnp.stack(tile_list, axis=1)


def plain_body(voltages, filter_taps, input_gain, input_flags, kept_channels, tile_order):
    local_inputs, padded_frames, samples = voltages.shape
    tap_count = filter_taps.shape[0]
    frames = padded_frames - tap_count + 1
    kept = kept_channels.shape[0]
    table = dft_table(kept_channels, samples)
    filtered = jnp.zeros((local_inputs, frames, samples), jnp.float32)
    for tap_index in range(tap_count):
        filtered = filtered + voltages[:, tap_index : tap_index + frames, :].astype(
            jnp.float32
        ) * filter_taps[tap_index].astype(jnp.float32)
    filtered = (filtered * input_gain[:, None, None]).astype(jnp.bfloat16)
    spectra = jnp.dot(
        filtered.reshape(local_inputs * frames, samples), table, preferred_element_type=jnp.float32
    )
    weights = jnp.repeat(input_flags.astype(jnp.float32), frames)[:, None]
    spectra = spectra * weights
    squares = spectra[:, :kept] * spectra[:, :kept] + spectra[:, kept:] * spectra[:, kept:]
    total_power = lax.psum(jnp.sum(squares, axis=0), "wide")
    all_inputs = local_inputs * lax.axis_size("wide")
    power = total_power / jnp.float32(all_inputs * frames) + jnp.float32(eps_power)
    scale = lax.rsqrt(power)
    equalized = (spectra * jnp.concatenate([scale, scale])[None, :]).astype(jnp.bfloat16)
    arranged = equalized.reshape(local_inputs, frames, 2, kept).transpose(3, 2, 1, 0)
    turned = lax.all_to_all(arranged, "wide", split_axis=0, concat_axis=3, tiled=True)
    summed = visibility_terms(turned, tile_order, BLK)
    return (summed * jnp.float32(1.0 / frames)).astype(jnp.bfloat16)


LANES = 128
CHUNK = 16
PIECES = 4
GROUPS = 2
PRESCALE = 1024.0


def dft_rows(kept_channels, samples):
    fine = LANES
    step = jnp.float32(2.0 * math.pi / samples)
    high = jnp.arange(samples // fine, dtype=jnp.int32) * fine
    low = jnp.arange(fine, dtype=jnp.int32)
    angle_h = (kept_channels[:, None] * high[None, :] % samples).astype(jnp.float32) * step
    angle_l = (kept_channels[:, None] * low[None, :] % samples).astype(jnp.float32) * step
    factor = jnp.float32(1.0 / math.sqrt(samples / 2))
    cos_h, sin_h = jnp.cos(angle_h) * factor, jnp.sin(angle_h) * factor
    cos_l, sin_l = jnp.cos(angle_l), jnp.sin(angle_l)
    rows = []
    for step_index in range(samples // fine):
        ch = cos_h[:, step_index : step_index + 1]
        sh = sin_h[:, step_index : step_index + 1]
        rows.append((ch * cos_l - sh * sin_l, -(sh * cos_l + ch * sin_l)))
    real = jnp.concatenate([r for r, _ in rows], axis=1)
    imag = jnp.concatenate([m for _, m in rows], axis=1)
    return jnp.stack([real, imag], axis=1).reshape(-1, samples).astype(jnp.bfloat16)


def filter_kernel(main, h0, h1, h2, taps, gain, weight, table, *rest):
    groups = len(rest) - 2
    outs, filt, turn = rest[:groups], rest[groups], rest[groups + 1]
    sub = pl.program_id(0)
    inputs = main.shape[1]
    halos = (h0, h1, h2)

    @pl.loop(0, main.shape[2] // LANES)
    def _(strip):
        cols = pl.ds(pl.multiple_of(strip * LANES, LANES), LANES)
        tap_rows = [jnp.broadcast_to(taps[t : t + 1, cols], (16, LANES)) for t in range(4)]
        for a in range(0, inputs, 16):
            g = gain[a : a + 16, :]
            window = [main[f, a : a + 16, cols].astype(jnp.float32) for f in range(3)]
            for f in range(CHUNK):
                if f + 3 < CHUNK:
                    newest = main[f + 3, a : a + 16, cols]
                else:
                    newest = halos[f + 3 - CHUNK][0, a : a + 16, cols]
                window.append(newest.astype(jnp.float32))
                total = window[0] * tap_rows[0]
                for t in range(1, 4):
                    total = total + window[t] * tap_rows[t]
                filt[f * inputs + a : f * inputs + a + 16, cols] = (total * g).astype(jnp.bfloat16)
                window = window[1:]

    spectra = lax.dot_general(
        table[...], filt[...], (((1,), (1,)), ((), ())), preferred_element_type=jnp.float32
    )
    lane_rows = CHUNK * inputs // LANES
    height = 2 * lane_rows
    w = weight[...]
    channels = table.shape[0]
    for j in range(2):
        @pl.when(sub == j)
        def _():
            for r in range(lane_rows):
                turn[pl.ds(j * lane_rows + r, channels, stride=height), :] = (
                    spectra[:, r * LANES : (r + 1) * LANES] * w
                )

    @pl.when(sub == 1)
    def _():
        dests, local, _, _, _ = outs[0].shape
        every = local * groups

        @pl.loop(0, dests)
        def _(d):
            for g in range(groups):
                start = (d * every + g * local) * 2 * height
                block = turn[pl.ds(pl.multiple_of(start, 2 * height), local * 2 * height), :]
                outs[g][d] = block.astype(jnp.bfloat16).reshape(local, 2, height, LANES)


def filter_piece(piece, turned, taps, gain, weight, table, dests):
    _, inputs, samples = turned.shape
    channels = table.shape[0]
    local = channels // 2 // dests // GROUPS
    height = 2 * CHUNK * inputs // LANES
    shape = jax.ShapeDtypeStruct((dests, local, 2, height, LANES), jnp.bfloat16)
    halo = [
        pl.BlockSpec((1, inputs, samples), lambda i, j=j: ((piece * 2 + i + 1) * CHUNK + j, 0, 0))
        for j in range(3)
    ]
    whole = lambda x: pl.BlockSpec(x.shape, lambda i: (0, 0))
    return pl.pallas_call(
        filter_kernel,
        grid=(2,),
        in_specs=[pl.BlockSpec((CHUNK, inputs, samples), lambda i: (piece * 2 + i, 0, 0))]
        + halo
        + [whole(taps), whole(gain), whole(weight), whole(table)],
        out_specs=[pl.BlockSpec(shape.shape, lambda i: (0, 0, 0, 0, 0))] * GROUPS,
        out_shape=[shape] * GROUPS,
        scratch_shapes=[
            pltpu.VMEM((CHUNK * inputs, samples), jnp.bfloat16),
            pltpu.VMEM((channels * height, LANES), jnp.float32),
        ],
        compiler_params=pltpu.CompilerParams(vmem_limit_bytes=52 * 2**20),
        cost_estimate=pl.CostEstimate(
            flops=2 * 2 * CHUNK * inputs * samples * channels,
            bytes_accessed=2 * (CHUNK + 3) * inputs * samples * 2 + 6 * 2**20,
            transcendentals=0,
        ),
        name="filterbank",
    )(turned, turned, turned, turned, taps, gain, weight, table)


def correlate_kernel(slots, *rest, block, frames):
    pieces = rest[: PIECES]
    out, stacked, rotated, flipped = rest[PIECES:]
    sources, _, _, height, _ = pieces[0].shape
    half = LANES // 2
    for p in range(PIECES):
        for part in range(2):
            for s in range(0, sources, 2):
                first = pieces[p][s, 0, part]
                second = pieces[p][s + 1, 0, part]
                row = part * frames + p * 2 * height
                cols = slice(s * half, s * half + LANES)
                stacked[row : row + height, cols] = jnp.concatenate(
                    [first[:, :half], second[:, :half]], axis=1
                )
                stacked[row + height : row + 2 * height, cols] = jnp.concatenate(
                    [first[:, half:], second[:, half:]], axis=1
                )
    inputs = stacked.shape[1]
    x = stacked[...].astype(jnp.float32)
    total = jnp.sum(x * x, keepdims=True)
    power = total / jnp.float32(inputs * frames * PRESCALE * PRESCALE) + jnp.float32(eps_power)
    scale = lax.rsqrt(power)
    scale = scale * scale * jnp.float32(1.0 / (frames * PRESCALE * PRESCALE))
    flipped[...] = stacked[...].T
    rotated[:frames, :] = -stacked[frames:, :]
    rotated[frames:, :] = stacked[:frames, :]
    blocks = inputs // block
    row_table, col_table = tile_tables(blocks)
    for c in range(blocks):
        cols = slice(c * block, (c + 1) * block)
        for r in range(c + 1):
            tile = [t for t in range(len(row_table)) if row_table[t] == r and col_table[t] == c][0]
            slot = slots[tile]
            left = flipped[r * block : (r + 1) * block, :]
            for part, right in ((0, stacked), (1, rotated)):
                gram = jnp.dot(left, right[:, cols], preferred_element_type=jnp.float32)
                out[0, slot, part] = (gram * scale).astype(jnp.bfloat16)


def correlate(slots, pieces, offset, total, previous):
    sources, local, _, height, _ = pieces[0].shape
    inputs = sources * LANES // 2
    frames = PIECES * height * 2
    tiles = slots.shape[0]
    in_specs = [pl.BlockSpec((sources, 1, 2, height, LANES), lambda k, *_: (0, k, 0, 0, 0))] * PIECES
    operands = [slots, *pieces]
    kernel = functools.partial(correlate_kernel, block=BLK, frames=frames)
    aliases = {}
    if previous is not None:
        base = kernel
        kernel = lambda s, prev, *rest: base(s, *rest)
        in_specs = [pl.BlockSpec(memory_space=pl.ANY)] + in_specs
        operands = [slots, previous, *pieces]
        aliases = {1: 0}
    return pl.pallas_call(
        kernel,
        grid_spec=pltpu.PrefetchScalarGridSpec(
            num_scalar_prefetch=1,
            grid=(local,),
            in_specs=in_specs,
            out_specs=pl.BlockSpec(
                (1, tiles, 2, BLK, BLK), lambda k, *_: (k + offset, 0, 0, 0, 0)
            ),
            scratch_shapes=[
                pltpu.VMEM((2 * frames, inputs), jnp.bfloat16),
                pltpu.VMEM((2 * frames, inputs), jnp.bfloat16),
                pltpu.VMEM((inputs, 2 * frames), jnp.bfloat16),
            ],
        ),
        out_shape=jax.ShapeDtypeStruct((total, tiles, 2, BLK, BLK), jnp.bfloat16),
        input_output_aliases=aliases,
        compiler_params=pltpu.CompilerParams(vmem_limit_bytes=40 * 2**20),
        cost_estimate=pl.CostEstimate(
            flops=local * tiles * 2 * 2 * BLK * BLK * 2 * frames,
            bytes_accessed=local * (tiles * 2 * BLK * BLK * 2 + inputs * frames * 4),
            transcendentals=0,
        ),
        name="correlate",
    )(*operands)


def body(voltages, filter_taps, input_gain, input_flags, kept_channels, tile_order):
    local_inputs, padded_frames, samples = voltages.shape
    taps = filter_taps.shape[0]
    frames = padded_frames - taps + 1
    kept = kept_channels.shape[0]
    devices = lax.axis_size("wide")
    fits = (
        local_inputs * 2 == LANES
        and taps == 4
        and frames == PIECES * 2 * CHUNK
        and devices % 2 == 0
        and kept % (devices * GROUPS) == 0
        and samples % LANES == 0
    )
    if not fits:
        return plain_body(
            voltages, filter_taps, input_gain, input_flags, kept_channels, tile_order
        )
    table = dft_rows(kept_channels, samples)
    turned = jnp.transpose(voltages, (1, 0, 2))
    gain = jnp.broadcast_to(input_gain[:, None], (local_inputs, LANES))
    weight = input_flags.astype(jnp.float32) * jnp.float32(PRESCALE)
    weight = jnp.concatenate([weight, weight])[None, :]
    float_taps = filter_taps.astype(jnp.float32)
    tiles = tile_order.shape[0]
    numbers = jnp.arange(tiles, dtype=jnp.int32)
    slots = jnp.sum(
        jnp.where(tile_order[None, :] == numbers[:, None], numbers[None, :], 0), axis=1
    ).astype(jnp.int32)
    received = [[] for _ in range(GROUPS)]
    for piece in range(PIECES):
        outs = filter_piece(piece, turned, float_taps, gain, weight, table, devices)
        for g in range(GROUPS):
            received[g].append(
                lax.all_to_all(outs[g], "wide", split_axis=0, concat_axis=0, tiled=True)
            )
    local = kept // devices
    result = None
    for g in range(GROUPS):
        result = correlate(slots, received[g], g * (local // GROUPS), local, result)
    return result


def solution(mesh):
    return jax.shard_map(
        body,
        mesh=mesh,
        in_specs=(
            P(("grp", "wide"), None, None),
            P(),
            P(("grp", "wide")),
            P(("grp", "wide")),
            P(),
            P(),
        ),
        out_specs=P(("grp", "wide"), None, None, None, None),
        check_vma=False,
    )
```

```python
import functools
import math

import jax
import jax.numpy as jnp
import numpy as np
from jax import lax
from jax.experimental import pallas as pl
from jax.experimental.pallas import tpu as pltpu
from jax.sharding import PartitionSpec as P

BLK = 256


eps_power = 1e-06


def tile_tables(blocks):
    row_list = []
    col_list = []
    for row_block in range(blocks):
        for col_block in range(row_block, blocks):
            row_list.append(row_block)
            col_list.append(col_block)
    return (np.array(row_list, np.int32), np.array(col_list, np.int32))


def dft_table(kept_channels, samples):
    sample_index = jnp.arange(samples, dtype=jnp.int32)
    product = sample_index[:, None] * kept_channels[None, :] % samples
    phase = product.astype(jnp.float32) * jnp.float32(2.0 * math.pi / samples)
    factor = jnp.float32(1.0 / math.sqrt(samples / 2))
    return jnp.concatenate([jnp.cos(phase) * factor, -jnp.sin(phase) * factor], axis=1).astype(
        jnp.bfloat16
    )


def tile_corner(tile_order, slot_index, corner_table):
    picked = tile_order[slot_index] == jnp.arange(corner_table.shape[0], dtype=jnp.int32)
    return jnp.sum(jnp.where(picked, jnp.asarray(corner_table), 0)).astype(jnp.int32)


def visibility_terms(turned, tile_order, block_size):
    real_part = turned[:, 0]
    imag_part = turned[:, 1]
    stacked = jnp.concatenate([real_part, imag_part], axis=1)
    rotated = jnp.concatenate([imag_part, -real_part], axis=1)
    local_channels = turned.shape[0]
    row_table, col_table = tile_tables(turned.shape[3] // block_size)
    tile_list = []
    real_full = jnp.einsum("cfi,cfj->cij", stacked, stacked, preferred_element_type=jnp.float32)
    imag_full = jnp.einsum("cfi,cfj->cij", rotated, stacked, preferred_element_type=jnp.float32)
    for slot_index in range(row_table.shape[0]):
        row_start = tile_corner(tile_order, slot_index, row_table) * block_size
        col_start = tile_corner(tile_order, slot_index, col_table) * block_size
        zero_start = jnp.zeros((), jnp.int32)
        real_tile = lax.dynamic_slice(
            real_full, (zero_start, row_start, col_start), (local_channels, block_size, block_size)
        )
        imag_tile = lax.dynamic_slice(
            imag_full, (zero_start, row_start, col_start), (local_channels, block_size, block_size)
        )
        tile_list.append(jnp.stack([real_tile, imag_tile], axis=1))
    return jnp.stack(tile_list, axis=1)


def plain_body(voltages, filter_taps, input_gain, input_flags, kept_channels, tile_order):
    local_inputs, padded_frames, samples = voltages.shape
    tap_count = filter_taps.shape[0]
    frames = padded_frames - tap_count + 1
    kept = kept_channels.shape[0]
    table = dft_table(kept_channels, samples)
    filtered = jnp.zeros((local_inputs, frames, samples), jnp.float32)
    for tap_index in range(tap_count):
        filtered = filtered + voltages[:, tap_index : tap_index + frames, :].astype(
            jnp.float32
        ) * filter_taps[tap_index].astype(jnp.float32)
    filtered = (filtered * input_gain[:, None, None]).astype(jnp.bfloat16)
    spectra = jnp.dot(
        filtered.reshape(local_inputs * frames, samples), table, preferred_element_type=jnp.float32
    )
    weights = jnp.repeat(input_flags.astype(jnp.float32), frames)[:, None]
    spectra = spectra * weights
    squares = spectra[:, :kept] * spectra[:, :kept] + spectra[:, kept:] * spectra[:, kept:]
    total_power = lax.psum(jnp.sum(squares, axis=0), "wide")
    all_inputs = local_inputs * lax.axis_size("wide")
    power = total_power / jnp.float32(all_inputs * frames) + jnp.float32(eps_power)
    scale = lax.rsqrt(power)
    equalized = (spectra * jnp.concatenate([scale, scale])[None, :]).astype(jnp.bfloat16)
    arranged = equalized.reshape(local_inputs, frames, 2, kept).transpose(3, 2, 1, 0)
    turned = lax.all_to_all(arranged, "wide", split_axis=0, concat_axis=3, tiled=True)
    summed = visibility_terms(turned, tile_order, BLK)
    return (summed * jnp.float32(1.0 / frames)).astype(jnp.bfloat16)


LANES = 128
CHUNK = 16
PIECES = 4
GROUPS = 1
PRESCALE = 1024.0


def dft_rows(kept_channels, samples):
    fine = LANES
    step = jnp.float32(2.0 * math.pi / samples)
    high = jnp.arange(samples // fine, dtype=jnp.int32) * fine
    low = jnp.arange(fine, dtype=jnp.int32)
    angle_h = (kept_channels[:, None] * high[None, :] % samples).astype(jnp.float32) * step
    angle_l = (kept_channels[:, None] * low[None, :] % samples).astype(jnp.float32) * step
    factor = jnp.float32(1.0 / math.sqrt(samples / 2))
    cos_h, sin_h = jnp.cos(angle_h) * factor, jnp.sin(angle_h) * factor
    cos_l, sin_l = jnp.cos(angle_l), jnp.sin(angle_l)
    cos_h, sin_h, cos_l, sin_l = lax.optimization_barrier((cos_h, sin_h, cos_l, sin_l))
    rows = []
    for step_index in range(samples // fine):
        ch = cos_h[:, step_index : step_index + 1]
        sh = sin_h[:, step_index : step_index + 1]
        rows.append((ch * cos_l - sh * sin_l, -(sh * cos_l + ch * sin_l)))
    real = jnp.concatenate([r for r, _ in rows], axis=1)
    imag = jnp.concatenate([m for _, m in rows], axis=1)
    return jnp.stack([real, imag], axis=1).reshape(-1, samples).astype(jnp.bfloat16)


def filter_kernel(main, h0, h1, h2, taps, gain, weight, table, *rest):
    groups = len(rest) - 2
    outs, filt, turn = rest[:groups], rest[groups], rest[groups + 1]
    sub = pl.program_id(0)
    inputs = main.shape[1]
    halos = (h0, h1, h2)

    @pl.loop(0, main.shape[2] // LANES)
    def _(strip):
        cols = pl.ds(pl.multiple_of(strip * LANES, LANES), LANES)
        tap_rows = [jnp.broadcast_to(taps[t : t + 1, cols], (16, LANES)) for t in range(4)]
        for a in range(0, inputs, 16):
            g = gain[a : a + 16, :]
            window = [main[f, a : a + 16, cols].astype(jnp.float32) for f in range(3)]
            for f in range(CHUNK):
                if f + 3 < CHUNK:
                    newest = main[f + 3, a : a + 16, cols]
                else:
                    newest = halos[f + 3 - CHUNK][0, a : a + 16, cols]
                window.append(newest.astype(jnp.float32))
                total = window[0] * tap_rows[0]
                for t in range(1, 4):
                    total = total + window[t] * tap_rows[t]
                filt[f * inputs + a : f * inputs + a + 16, cols] = (total * g).astype(jnp.bfloat16)
                window = window[1:]

    spectra = lax.dot_general(
        table[...], filt[...], (((1,), (1,)), ((), ())), preferred_element_type=jnp.float32
    )
    lane_rows = CHUNK * inputs // LANES
    height = 2 * lane_rows
    w = weight[...]
    channels = table.shape[0]
    for j in range(2):
        @pl.when(sub == j)
        def _():
            for r in range(lane_rows):
                turn[pl.ds(j * lane_rows + r, channels, stride=height), :] = (
                    spectra[:, r * LANES : (r + 1) * LANES] * w
                )

    @pl.when(sub == 1)
    def _():
        dests, local, _, _, _ = outs[0].shape
        every = local * groups

        @pl.loop(0, dests)
        def _(d):
            for g in range(groups):
                start = (d * every + g * local) * 2 * height
                block = turn[pl.ds(pl.multiple_of(start, 2 * height), local * 2 * height), :]
                outs[g][d] = block.astype(jnp.bfloat16).reshape(local, 2, height, LANES)


def filter_piece(piece, turned, taps, gain, weight, table, dests):
    _, inputs, samples = turned.shape
    channels = table.shape[0]
    local = channels // 2 // dests // GROUPS
    height = 2 * CHUNK * inputs // LANES
    shape = jax.ShapeDtypeStruct((dests, local, 2, height, LANES), jnp.bfloat16)
    halo = [
        pl.BlockSpec((1, inputs, samples), lambda i, j=j: ((piece * 2 + i + 1) * CHUNK + j, 0, 0))
        for j in range(3)
    ]
    whole = lambda x: pl.BlockSpec(x.shape, lambda i: (0, 0))
    return pl.pallas_call(
        filter_kernel,
        grid=(2,),
        in_specs=[pl.BlockSpec((CHUNK, inputs, samples), lambda i: (piece * 2 + i, 0, 0))]
        + halo
        + [whole(taps), whole(gain), whole(weight), whole(table)],
        out_specs=[pl.BlockSpec(shape.shape, lambda i: (0, 0, 0, 0, 0))] * GROUPS,
        out_shape=[shape] * GROUPS,
        scratch_shapes=[
            pltpu.VMEM((CHUNK * inputs, samples), jnp.bfloat16),
            pltpu.VMEM((channels * height, LANES), jnp.float32),
        ],
        compiler_params=pltpu.CompilerParams(vmem_limit_bytes=52 * 2**20),
        cost_estimate=pl.CostEstimate(
            flops=2 * 2 * CHUNK * inputs * samples * channels,
            bytes_accessed=2 * (CHUNK + 3) * inputs * samples * 2 + 6 * 2**20,
            transcendentals=0,
        ),
        name="filterbank",
    )(turned, turned, turned, turned, taps, gain, weight, table)


def correlate_kernel(slots, *rest, block, frames):
    pieces = rest[: PIECES]
    out, stacked, rotated, flipped = rest[PIECES:]
    sources, _, _, height, _ = pieces[0].shape
    half = LANES // 2
    for p in range(PIECES):
        for part in range(2):
            for s in range(0, sources, 2):
                first = pieces[p][s, 0, part]
                second = pieces[p][s + 1, 0, part]
                row = part * frames + p * 2 * height
                cols = slice(s * half, s * half + LANES)
                stacked[row : row + height, cols] = jnp.concatenate(
                    [first[:, :half], second[:, :half]], axis=1
                )
                stacked[row + height : row + 2 * height, cols] = jnp.concatenate(
                    [first[:, half:], second[:, half:]], axis=1
                )
    inputs = stacked.shape[1]
    x = stacked[...].astype(jnp.float32)
    total = jnp.sum(x * x, keepdims=True)
    power = total / jnp.float32(inputs * frames * PRESCALE * PRESCALE) + jnp.float32(eps_power)
    scale = lax.rsqrt(power)
    scale = scale * scale * jnp.float32(1.0 / (frames * PRESCALE * PRESCALE))
    flipped[...] = stacked[...].T
    rotated[:frames, :] = -stacked[frames:, :]
    rotated[frames:, :] = stacked[:frames, :]
    blocks = inputs // block
    row_table, col_table = tile_tables(blocks)
    for c in range(blocks):
        cols = slice(c * block, (c + 1) * block)
        for r in range(c + 1):
            tile = [t for t in range(len(row_table)) if row_table[t] == r and col_table[t] == c][0]
            slot = slots[tile]
            left = flipped[r * block : (r + 1) * block, :]
            for part, right in ((0, stacked), (1, rotated)):
                gram = jnp.dot(left, right[:, cols], preferred_element_type=jnp.float32)
                out[0, slot, part] = (gram * scale).astype(jnp.bfloat16)


def correlate(slots, pieces, offset, total, previous):
    sources, local, _, height, _ = pieces[0].shape
    inputs = sources * LANES // 2
    frames = PIECES * height * 2
    tiles = slots.shape[0]
    in_specs = [pl.BlockSpec((sources, 1, 2, height, LANES), lambda k, *_: (0, k, 0, 0, 0))] * PIECES
    operands = [slots, *pieces]
    kernel = functools.partial(correlate_kernel, block=BLK, frames=frames)
    aliases = {}
    if previous is not None:
        base = kernel
        kernel = lambda s, prev, *rest: base(s, *rest)
        in_specs = [pl.BlockSpec(memory_space=pl.ANY)] + in_specs
        operands = [slots, previous, *pieces]
        aliases = {1: 0}
    return pl.pallas_call(
        kernel,
        grid_spec=pltpu.PrefetchScalarGridSpec(
            num_scalar_prefetch=1,
            grid=(local,),
            in_specs=in_specs,
            out_specs=pl.BlockSpec(
                (1, tiles, 2, BLK, BLK), lambda k, *_: (k + offset, 0, 0, 0, 0)
            ),
            scratch_shapes=[
                pltpu.VMEM((2 * frames, inputs), jnp.bfloat16),
                pltpu.VMEM((2 * frames, inputs), jnp.bfloat16),
                pltpu.VMEM((inputs, 2 * frames), jnp.bfloat16),
            ],
        ),
        out_shape=jax.ShapeDtypeStruct((total, tiles, 2, BLK, BLK), jnp.bfloat16),
        input_output_aliases=aliases,
        compiler_params=pltpu.CompilerParams(vmem_limit_bytes=40 * 2**20),
        cost_estimate=pl.CostEstimate(
            flops=local * tiles * 2 * 2 * BLK * BLK * 2 * frames,
            bytes_accessed=local * (tiles * 2 * BLK * BLK * 2 + inputs * frames * 4),
            transcendentals=0,
        ),
        name="correlate",
    )(*operands)


def body(voltages, filter_taps, input_gain, input_flags, kept_channels, tile_order):
    local_inputs, padded_frames, samples = voltages.shape
    taps = filter_taps.shape[0]
    frames = padded_frames - taps + 1
    kept = kept_channels.shape[0]
    devices = lax.axis_size("wide")
    fits = (
        local_inputs * 2 == LANES
        and taps == 4
        and frames == PIECES * 2 * CHUNK
        and devices % 2 == 0
        and kept % (devices * GROUPS) == 0
        and samples % LANES == 0
    )
    if not fits:
        return plain_body(
            voltages, filter_taps, input_gain, input_flags, kept_channels, tile_order
        )
    table = dft_rows(kept_channels, samples)
    turned = jnp.transpose(voltages, (1, 0, 2))
    gain = jnp.broadcast_to(input_gain[:, None], (local_inputs, LANES))
    weight = input_flags.astype(jnp.float32) * jnp.float32(PRESCALE)
    weight = jnp.concatenate([weight, weight])[None, :]
    float_taps = filter_taps.astype(jnp.float32)
    tiles = tile_order.shape[0]
    numbers = jnp.arange(tiles, dtype=jnp.int32)
    slots = jnp.sum(
        jnp.where(tile_order[None, :] == numbers[:, None], numbers[None, :], 0), axis=1
    ).astype(jnp.int32)
    received = [[] for _ in range(GROUPS)]
    for piece in range(PIECES):
        outs = filter_piece(piece, turned, float_taps, gain, weight, table, devices)
        for g in range(GROUPS):
            received[g].append(
                lax.all_to_all(outs[g], "wide", split_axis=0, concat_axis=0, tiled=True)
            )
    local = kept // devices
    result = None
    for g in range(GROUPS):
        result = correlate(slots, received[g], g * (local // GROUPS), local, result)
    return result


def solution(mesh):
    return jax.shard_map(
        body,
        mesh=mesh,
        in_specs=(
            P(("grp", "wide"), None, None),
            P(),
            P(("grp", "wide")),
            P(("grp", "wide")),
            P(),
            P(),
        ),
        out_specs=P(("grp", "wide"), None, None, None, None),
        check_vma=False,
    )
```

```python
import functools
import math

import jax
import jax.numpy as jnp
import numpy as np
from jax import lax
from jax.experimental import pallas as pl
from jax.experimental.pallas import tpu as pltpu
from jax.sharding import PartitionSpec as P

BLK = 256


eps_power = 1e-06


def tile_tables(blocks):
    row_list = []
    col_list = []
    for row_block in range(blocks):
        for col_block in range(row_block, blocks):
            row_list.append(row_block)
            col_list.append(col_block)
    return (np.array(row_list, np.int32), np.array(col_list, np.int32))


def dft_table(kept_channels, samples):
    sample_index = jnp.arange(samples, dtype=jnp.int32)
    product = sample_index[:, None] * kept_channels[None, :] % samples
    phase = product.astype(jnp.float32) * jnp.float32(2.0 * math.pi / samples)
    factor = jnp.float32(1.0 / math.sqrt(samples / 2))
    return jnp.concatenate([jnp.cos(phase) * factor, -jnp.sin(phase) * factor], axis=1).astype(
        jnp.bfloat16
    )


def tile_corner(tile_order, slot_index, corner_table):
    picked = tile_order[slot_index] == jnp.arange(corner_table.shape[0], dtype=jnp.int32)
    return jnp.sum(jnp.where(picked, jnp.asarray(corner_table), 0)).astype(jnp.int32)


def visibility_terms(turned, tile_order, block_size):
    real_part = turned[:, 0]
    imag_part = turned[:, 1]
    stacked = jnp.concatenate([real_part, imag_part], axis=1)
    rotated = jnp.concatenate([imag_part, -real_part], axis=1)
    local_channels = turned.shape[0]
    row_table, col_table = tile_tables(turned.shape[3] // block_size)
    tile_list = []
    real_full = jnp.einsum("cfi,cfj->cij", stacked, stacked, preferred_element_type=jnp.float32)
    imag_full = jnp.einsum("cfi,cfj->cij", rotated, stacked, preferred_element_type=jnp.float32)
    for slot_index in range(row_table.shape[0]):
        row_start = tile_corner(tile_order, slot_index, row_table) * block_size
        col_start = tile_corner(tile_order, slot_index, col_table) * block_size
        zero_start = jnp.zeros((), jnp.int32)
        real_tile = lax.dynamic_slice(
            real_full, (zero_start, row_start, col_start), (local_channels, block_size, block_size)
        )
        imag_tile = lax.dynamic_slice(
            imag_full, (zero_start, row_start, col_start), (local_channels, block_size, block_size)
        )
        tile_list.append(jnp.stack([real_tile, imag_tile], axis=1))
    return jnp.stack(tile_list, axis=1)


def plain_body(voltages, filter_taps, input_gain, input_flags, kept_channels, tile_order):
    local_inputs, padded_frames, samples = voltages.shape
    tap_count = filter_taps.shape[0]
    frames = padded_frames - tap_count + 1
    kept = kept_channels.shape[0]
    table = dft_table(kept_channels, samples)
    filtered = jnp.zeros((local_inputs, frames, samples), jnp.float32)
    for tap_index in range(tap_count):
        filtered = filtered + voltages[:, tap_index : tap_index + frames, :].astype(
            jnp.float32
        ) * filter_taps[tap_index].astype(jnp.float32)
    filtered = (filtered * input_gain[:, None, None]).astype(jnp.bfloat16)
    spectra = jnp.dot(
        filtered.reshape(local_inputs * frames, samples), table, preferred_element_type=jnp.float32
    )
    weights = jnp.repeat(input_flags.astype(jnp.float32), frames)[:, None]
    spectra = spectra * weights
    squares = spectra[:, :kept] * spectra[:, :kept] + spectra[:, kept:] * spectra[:, kept:]
    total_power = lax.psum(jnp.sum(squares, axis=0), "wide")
    all_inputs = local_inputs * lax.axis_size("wide")
    power = total_power / jnp.float32(all_inputs * frames) + jnp.float32(eps_power)
    scale = lax.rsqrt(power)
    equalized = (spectra * jnp.concatenate([scale, scale])[None, :]).astype(jnp.bfloat16)
    arranged = equalized.reshape(local_inputs, frames, 2, kept).transpose(3, 2, 1, 0)
    turned = lax.all_to_all(arranged, "wide", split_axis=0, concat_axis=3, tiled=True)
    summed = visibility_terms(turned, tile_order, BLK)
    return (summed * jnp.float32(1.0 / frames)).astype(jnp.bfloat16)


LANES = 128
CHUNK = 16
PIECES = 4
PRESCALE = 1024.0


def dft_rows(kept_channels, samples):
    fine = LANES
    step = jnp.float32(2.0 * math.pi / samples)
    high = jnp.arange(samples // fine, dtype=jnp.int32) * fine
    low = jnp.arange(fine, dtype=jnp.int32)
    angle_h = (kept_channels[:, None] * high[None, :] % samples).astype(jnp.float32) * step
    angle_l = (kept_channels[:, None] * low[None, :] % samples).astype(jnp.float32) * step
    factor = jnp.float32(1.0 / math.sqrt(samples / 2))
    cos_h, sin_h = jnp.cos(angle_h) * factor, jnp.sin(angle_h) * factor
    cos_l, sin_l = jnp.cos(angle_l), jnp.sin(angle_l)
    cos_h, sin_h, cos_l, sin_l = lax.optimization_barrier((cos_h, sin_h, cos_l, sin_l))
    rows = []
    for step_index in range(samples // fine):
        ch = cos_h[:, step_index : step_index + 1]
        sh = sin_h[:, step_index : step_index + 1]
        rows.append((ch * cos_l - sh * sin_l, -(sh * cos_l + ch * sin_l)))
    real = jnp.concatenate([r for r, _ in rows], axis=1)
    imag = jnp.concatenate([m for _, m in rows], axis=1)
    return jnp.stack([real, imag], axis=1).reshape(-1, samples).astype(jnp.bfloat16)


def filter_kernel(main, h0, h1, h2, taps, gain, weight, table, *rest):
    out, filt, turn, staged, send_sem, recv_sem, own_sem = rest
    step = pl.program_id(0)
    sub = lax.rem(step, 2)
    piece = lax.div(step, 2)
    me = lax.axis_index("wide")
    devices = out.shape[1]
    barrier = pltpu.get_barrier_semaphore()

    @pl.when(step == 0)
    def _():
        @pl.loop(1, devices)
        def _(o):
            pl.semaphore_signal(
                barrier,
                inc=1,
                device_id={"wide": lax.rem(me + o, devices)},
                device_id_type=pl.DeviceIdType.MESH,
            )

        pl.semaphore_wait(barrier, devices - 1)

    def remote(p, o, slot):
        peer = lax.rem(me + o, devices)
        return pltpu.make_async_remote_copy(
            src_ref=staged.at[p, peer],
            dst_ref=out.at[p, slot],
            send_sem=send_sem.at[p, o],
            recv_sem=recv_sem.at[p, o],
            device_id={"wide": peer},
            device_id_type=pl.DeviceIdType.MESH,
        )

    def own(p):
        return pltpu.make_async_copy(staged.at[p, me], out.at[p, me], own_sem.at[p])

    inputs = main.shape[1]
    halos = (h0, h1, h2)

    @pl.loop(0, main.shape[2] // LANES)
    def _(strip):
        cols = pl.ds(pl.multiple_of(strip * LANES, LANES), LANES)
        tap_rows = [jnp.broadcast_to(taps[t : t + 1, cols], (16, LANES)) for t in range(4)]
        for a in range(0, inputs, 16):
            g = gain[a : a + 16, :]
            window = [main[f, a : a + 16, cols].astype(jnp.float32) for f in range(3)]
            for f in range(CHUNK):
                if f + 3 < CHUNK:
                    newest = main[f + 3, a : a + 16, cols]
                else:
                    newest = halos[f + 3 - CHUNK][0, a : a + 16, cols]
                window.append(newest.astype(jnp.float32))
                total = window[0] * tap_rows[0]
                for t in range(1, 4):
                    total = total + window[t] * tap_rows[t]
                filt[f * inputs + a : f * inputs + a + 16, cols] = (total * g).astype(jnp.bfloat16)
                window = window[1:]

    spectra = lax.dot_general(
        table[...], filt[...], (((1,), (1,)), ((), ())), preferred_element_type=jnp.float32
    )
    lane_rows = CHUNK * inputs // LANES
    height = 2 * lane_rows
    w = weight[...]
    channels = table.shape[0]
    for j in range(2):
        @pl.when(sub == j)
        def _():
            for r in range(lane_rows):
                turn[pl.ds(j * lane_rows + r, channels, stride=height), :] = (
                    spectra[:, r * LANES : (r + 1) * LANES] * w
                )

    local = out.shape[2]

    def stage(d):
        rows = local * 2 * height
        block = turn[pl.ds(pl.multiple_of(d * rows, rows), rows), :]
        staged[piece, d] = block.astype(jnp.bfloat16).reshape(local, 2, height, LANES)

    @pl.when(sub == 1)
    def _():
        @pl.loop(1, devices)
        def _(o):
            stage(lax.rem(me + o, devices))
            remote(piece, o, me).start()

        stage(me)
        own(piece).start()

    @pl.when(step == 2 * PIECES - 1)
    def _():
        @pl.loop(0, PIECES)
        def _(p):
            own(p).wait()

            @pl.loop(1, devices)
            def _(o):
                remote(p, o, me).wait_send()
                remote(p, o, lax.rem(me - o + devices, devices)).wait_recv()


def filter_and_send(turned, taps, gain, weight, table, dests):
    _, inputs, samples = turned.shape
    channels = table.shape[0]
    local = channels // 2 // dests
    height = 2 * CHUNK * inputs // LANES
    shape = (PIECES, dests, local, 2, height, LANES)
    halo = [
        pl.BlockSpec((1, inputs, samples), lambda i, j=j: ((i + 1) * CHUNK + j, 0, 0))
        for j in range(3)
    ]
    whole = lambda x: pl.BlockSpec(x.shape, lambda i: (0, 0))
    return pl.pallas_call(
        filter_kernel,
        grid=(2 * PIECES,),
        in_specs=[pl.BlockSpec((CHUNK, inputs, samples), lambda i: (i, 0, 0))]
        + halo
        + [whole(taps), whole(gain), whole(weight), whole(table)],
        out_specs=pl.BlockSpec(memory_space=pl.ANY),
        out_shape=jax.ShapeDtypeStruct(shape, jnp.bfloat16),
        scratch_shapes=[
            pltpu.VMEM((CHUNK * inputs, samples), jnp.bfloat16),
            pltpu.VMEM((channels * height, LANES), jnp.float32),
            pltpu.VMEM(shape, jnp.bfloat16),
            pltpu.SemaphoreType.DMA((PIECES, dests)),
            pltpu.SemaphoreType.DMA((PIECES, dests)),
            pltpu.SemaphoreType.DMA((PIECES,)),
        ],
        compiler_params=pltpu.CompilerParams(
            vmem_limit_bytes=56 * 2**20, collective_id=0, has_side_effects=True
        ),
        name="filterbank_send",
    )(turned, turned, turned, turned, taps, gain, weight, table)


def correlate_kernel(slots, *rest, block, frames):
    received, out, stacked, rotated, flipped = rest
    _, sources, _, _, height, _ = received.shape
    half = LANES // 2
    for p in range(PIECES):
        for part in range(2):
            for s in range(0, sources, 2):
                first = received[p, s, 0, part]
                second = received[p, s + 1, 0, part]
                row = part * frames + p * 2 * height
                cols = slice(s * half, s * half + LANES)
                stacked[row : row + height, cols] = jnp.concatenate(
                    [first[:, :half], second[:, :half]], axis=1
                )
                stacked[row + height : row + 2 * height, cols] = jnp.concatenate(
                    [first[:, half:], second[:, half:]], axis=1
                )
    inputs = stacked.shape[1]
    x = stacked[...].astype(jnp.float32)
    total = jnp.sum(x * x, keepdims=True)
    power = total / jnp.float32(inputs * frames * PRESCALE * PRESCALE) + jnp.float32(eps_power)
    scale = lax.rsqrt(power)
    scale = scale * scale * jnp.float32(1.0 / (frames * PRESCALE * PRESCALE))
    flipped[...] = stacked[...].T
    rotated[:frames, :] = -stacked[frames:, :]
    rotated[frames:, :] = stacked[:frames, :]
    blocks = inputs // block
    row_table, col_table = tile_tables(blocks)
    for c in range(blocks):
        cols = slice(c * block, (c + 1) * block)
        for r in range(c + 1):
            tile = [t for t in range(len(row_table)) if row_table[t] == r and col_table[t] == c][0]
            slot = slots[tile]
            left = flipped[r * block : (r + 1) * block, :]
            for part, right in ((0, stacked), (1, rotated)):
                gram = jnp.dot(left, right[:, cols], preferred_element_type=jnp.float32)
                out[0, slot, part] = (gram * scale).astype(jnp.bfloat16)


def correlate(slots, received):
    _, sources, local, _, height, _ = received.shape
    inputs = sources * LANES // 2
    frames = PIECES * height * 2
    tiles = slots.shape[0]
    kernel = functools.partial(correlate_kernel, block=BLK, frames=frames)
    return pl.pallas_call(
        kernel,
        grid_spec=pltpu.PrefetchScalarGridSpec(
            num_scalar_prefetch=1,
            grid=(local,),
            in_specs=[
                pl.BlockSpec(
                    (PIECES, sources, 1, 2, height, LANES), lambda k, *_: (0, 0, k, 0, 0, 0)
                )
            ],
            out_specs=pl.BlockSpec(
                (1, tiles, 2, BLK, BLK), lambda k, *_: (k, 0, 0, 0, 0)
            ),
            scratch_shapes=[
                pltpu.VMEM((2 * frames, inputs), jnp.bfloat16),
                pltpu.VMEM((2 * frames, inputs), jnp.bfloat16),
                pltpu.VMEM((inputs, 2 * frames), jnp.bfloat16),
            ],
        ),
        out_shape=jax.ShapeDtypeStruct((local, tiles, 2, BLK, BLK), jnp.bfloat16),
        compiler_params=pltpu.CompilerParams(vmem_limit_bytes=40 * 2**20),
        cost_estimate=pl.CostEstimate(
            flops=local * tiles * 2 * 2 * BLK * BLK * 2 * frames,
            bytes_accessed=local * (tiles * 2 * BLK * BLK * 2 + inputs * frames * 4),
            transcendentals=0,
        ),
        name="correlate",
    )(slots, received)


def body(voltages, filter_taps, input_gain, input_flags, kept_channels, tile_order):
    local_inputs, padded_frames, samples = voltages.shape
    taps = filter_taps.shape[0]
    frames = padded_frames - taps + 1
    kept = kept_channels.shape[0]
    devices = lax.axis_size("wide")
    fits = (
        local_inputs * 2 == LANES
        and taps == 4
        and frames == PIECES * 2 * CHUNK
        and devices % 2 == 0
        and kept % devices == 0
        and samples % LANES == 0
    )
    if not fits:
        return plain_body(
            voltages, filter_taps, input_gain, input_flags, kept_channels, tile_order
        )
    table = dft_rows(kept_channels, samples)
    turned = jnp.transpose(voltages, (1, 0, 2))
    gain = jnp.broadcast_to(input_gain[:, None], (local_inputs, LANES))
    weight = input_flags.astype(jnp.float32) * jnp.float32(PRESCALE)
    weight = jnp.concatenate([weight, weight])[None, :]
    float_taps = filter_taps.astype(jnp.float32)
    tiles = tile_order.shape[0]
    numbers = jnp.arange(tiles, dtype=jnp.int32)
    slots = jnp.sum(
        jnp.where(tile_order[None, :] == numbers[:, None], numbers[None, :], 0), axis=1
    ).astype(jnp.int32)
    received = filter_and_send(turned, float_taps, gain, weight, table, devices)
    return correlate(slots, received)


def solution(mesh):
    return jax.shard_map(
        body,
        mesh=mesh,
        in_specs=(
            P(("grp", "wide"), None, None),
            P(),
            P(("grp", "wide")),
            P(("grp", "wide")),
            P(),
            P(),
        ),
        out_specs=P(("grp", "wide"), None, None, None, None),
        check_vma=False,
    )
```

```python
import functools
import math

import jax
import jax.numpy as jnp
import numpy as np
from jax import lax
from jax.experimental import pallas as pl
from jax.experimental.pallas import tpu as pltpu
from jax.sharding import PartitionSpec as P

BLK = 256


eps_power = 1e-06


def tile_tables(blocks):
    row_list = []
    col_list = []
    for row_block in range(blocks):
        for col_block in range(row_block, blocks):
            row_list.append(row_block)
            col_list.append(col_block)
    return (np.array(row_list, np.int32), np.array(col_list, np.int32))


def dft_table(kept_channels, samples):
    sample_index = jnp.arange(samples, dtype=jnp.int32)
    product = sample_index[:, None] * kept_channels[None, :] % samples
    phase = product.astype(jnp.float32) * jnp.float32(2.0 * math.pi / samples)
    factor = jnp.float32(1.0 / math.sqrt(samples / 2))
    return jnp.concatenate([jnp.cos(phase) * factor, -jnp.sin(phase) * factor], axis=1).astype(
        jnp.bfloat16
    )


def tile_corner(tile_order, slot_index, corner_table):
    picked = tile_order[slot_index] == jnp.arange(corner_table.shape[0], dtype=jnp.int32)
    return jnp.sum(jnp.where(picked, jnp.asarray(corner_table), 0)).astype(jnp.int32)


def visibility_terms(turned, tile_order, block_size):
    real_part = turned[:, 0]
    imag_part = turned[:, 1]
    stacked = jnp.concatenate([real_part, imag_part], axis=1)
    rotated = jnp.concatenate([imag_part, -real_part], axis=1)
    local_channels = turned.shape[0]
    row_table, col_table = tile_tables(turned.shape[3] // block_size)
    tile_list = []
    real_full = jnp.einsum("cfi,cfj->cij", stacked, stacked, preferred_element_type=jnp.float32)
    imag_full = jnp.einsum("cfi,cfj->cij", rotated, stacked, preferred_element_type=jnp.float32)
    for slot_index in range(row_table.shape[0]):
        row_start = tile_corner(tile_order, slot_index, row_table) * block_size
        col_start = tile_corner(tile_order, slot_index, col_table) * block_size
        zero_start = jnp.zeros((), jnp.int32)
        real_tile = lax.dynamic_slice(
            real_full, (zero_start, row_start, col_start), (local_channels, block_size, block_size)
        )
        imag_tile = lax.dynamic_slice(
            imag_full, (zero_start, row_start, col_start), (local_channels, block_size, block_size)
        )
        tile_list.append(jnp.stack([real_tile, imag_tile], axis=1))
    return jnp.stack(tile_list, axis=1)


def plain_body(voltages, filter_taps, input_gain, input_flags, kept_channels, tile_order):
    local_inputs, padded_frames, samples = voltages.shape
    tap_count = filter_taps.shape[0]
    frames = padded_frames - tap_count + 1
    kept = kept_channels.shape[0]
    table = dft_table(kept_channels, samples)
    filtered = jnp.zeros((local_inputs, frames, samples), jnp.float32)
    for tap_index in range(tap_count):
        filtered = filtered + voltages[:, tap_index : tap_index + frames, :].astype(
            jnp.float32
        ) * filter_taps[tap_index].astype(jnp.float32)
    filtered = (filtered * input_gain[:, None, None]).astype(jnp.bfloat16)
    spectra = jnp.dot(
        filtered.reshape(local_inputs * frames, samples), table, preferred_element_type=jnp.float32
    )
    weights = jnp.repeat(input_flags.astype(jnp.float32), frames)[:, None]
    spectra = spectra * weights
    squares = spectra[:, :kept] * spectra[:, :kept] + spectra[:, kept:] * spectra[:, kept:]
    total_power = lax.psum(jnp.sum(squares, axis=0), "wide")
    all_inputs = local_inputs * lax.axis_size("wide")
    power = total_power / jnp.float32(all_inputs * frames) + jnp.float32(eps_power)
    scale = lax.rsqrt(power)
    equalized = (spectra * jnp.concatenate([scale, scale])[None, :]).astype(jnp.bfloat16)
    arranged = equalized.reshape(local_inputs, frames, 2, kept).transpose(3, 2, 1, 0)
    turned = lax.all_to_all(arranged, "wide", split_axis=0, concat_axis=3, tiled=True)
    summed = visibility_terms(turned, tile_order, BLK)
    return (summed * jnp.float32(1.0 / frames)).astype(jnp.bfloat16)


LANES = 128
CHUNK = 16
PIECES = 4
PRESCALE = 1024.0


def dft_rows(kept_channels, samples):
    fine = LANES
    step = jnp.float32(2.0 * math.pi / samples)
    high = jnp.arange(samples // fine, dtype=jnp.int32) * fine
    low = jnp.arange(fine, dtype=jnp.int32)
    angle_h = (kept_channels[:, None] * high[None, :] % samples).astype(jnp.float32) * step
    angle_l = (kept_channels[:, None] * low[None, :] % samples).astype(jnp.float32) * step
    factor = jnp.float32(1.0 / math.sqrt(samples / 2))
    cos_h, sin_h = jnp.cos(angle_h) * factor, jnp.sin(angle_h) * factor
    cos_l, sin_l = jnp.cos(angle_l), jnp.sin(angle_l)
    cos_h, sin_h, cos_l, sin_l = lax.optimization_barrier((cos_h, sin_h, cos_l, sin_l))
    rows = []
    for step_index in range(samples // fine):
        ch = cos_h[:, step_index : step_index + 1]
        sh = sin_h[:, step_index : step_index + 1]
        rows.append((ch * cos_l - sh * sin_l, -(sh * cos_l + ch * sin_l)))
    real = jnp.concatenate([r for r, _ in rows], axis=1)
    imag = jnp.concatenate([m for _, m in rows], axis=1)
    return jnp.stack([real, imag], axis=1).reshape(-1, samples).astype(jnp.bfloat16)


def filter_kernel(main, h0, h1, h2, taps, gain, weight, table, *rest):
    out, filt, turn, staged, send_sem, recv_sem, own_sem = rest
    step = pl.program_id(0)
    sub = lax.rem(step, 2)
    piece = lax.div(step, 2)
    me = lax.axis_index("wide")
    devices = out.shape[1]
    barrier = pltpu.get_barrier_semaphore()

    @pl.when(step == 0)
    def _():
        @pl.loop(1, devices)
        def _(o):
            pl.semaphore_signal(
                barrier,
                inc=1,
                device_id={"wide": lax.rem(me + o, devices)},
                device_id_type=pl.DeviceIdType.MESH,
            )

        pl.semaphore_wait(barrier, devices - 1)

    def remote(p, o, slot):
        peer = lax.rem(me + o, devices)
        return pltpu.make_async_remote_copy(
            src_ref=staged.at[p, peer],
            dst_ref=out.at[p, slot],
            send_sem=send_sem.at[p, o],
            recv_sem=recv_sem.at[p, o],
            device_id={"wide": peer},
            device_id_type=pl.DeviceIdType.MESH,
        )

    def own(p):
        return pltpu.make_async_copy(staged.at[p, me], out.at[p, me], own_sem.at[p])

    inputs = main.shape[1]
    halos = (h0, h1, h2)

    @pl.loop(0, main.shape[2] // LANES)
    def _(strip):
        cols = pl.ds(pl.multiple_of(strip * LANES, LANES), LANES)
        tap_rows = [jnp.broadcast_to(taps[t : t + 1, cols], (16, LANES)) for t in range(4)]
        for a in range(0, inputs, 16):
            g = gain[a : a + 16, :]
            window = [main[f, a : a + 16, cols].astype(jnp.float32) for f in range(3)]
            for f in range(CHUNK):
                if f + 3 < CHUNK:
                    newest = main[f + 3, a : a + 16, cols]
                else:
                    newest = halos[f + 3 - CHUNK][0, a : a + 16, cols]
                window.append(newest.astype(jnp.float32))
                total = window[0] * tap_rows[0]
                for t in range(1, 4):
                    total = total + window[t] * tap_rows[t]
                filt[f * inputs + a : f * inputs + a + 16, cols] = (total * g).astype(jnp.bfloat16)
                window = window[1:]

    spectra = lax.dot_general(
        table[...], filt[...], (((1,), (1,)), ((), ())), preferred_element_type=jnp.float32
    )
    lane_rows = CHUNK * inputs // LANES
    height = 2 * lane_rows
    w = weight[...]
    channels = table.shape[0]
    for j in range(2):
        @pl.when(sub == j)
        def _():
            for r in range(lane_rows):
                turn[pl.ds(j * lane_rows + r, channels, stride=height), :] = (
                    spectra[:, r * LANES : (r + 1) * LANES] * w
                )

    local = out.shape[2]

    def stage(d):
        rows = local * 2 * height
        block = turn[pl.ds(pl.multiple_of(d * rows, rows), rows), :]
        staged[piece, d] = block.astype(jnp.bfloat16).reshape(local, 2, height, LANES)

    @pl.when(sub == 1)
    def _():
        @pl.loop(1, devices)
        def _(k):
            o = lax.rem(k + devices // 2 - 2, devices - 1) + 1
            stage(lax.rem(me + o, devices))
            remote(piece, o, me).start()

        stage(me)
        own(piece).start()

    @pl.when(step == 2 * PIECES - 1)
    def _():
        @pl.loop(0, PIECES)
        def _(p):
            own(p).wait()

            @pl.loop(1, devices)
            def _(o):
                remote(p, o, me).wait_send()
                remote(p, o, lax.rem(me - o + devices, devices)).wait_recv()


def filter_and_send(turned, taps, gain, weight, table, dests):
    _, inputs, samples = turned.shape
    channels = table.shape[0]
    local = channels // 2 // dests
    height = 2 * CHUNK * inputs // LANES
    shape = (PIECES, dests, local, 2, height, LANES)
    halo = [
        pl.BlockSpec((1, inputs, samples), lambda i, j=j: ((i + 1) * CHUNK + j, 0, 0))
        for j in range(3)
    ]
    whole = lambda x: pl.BlockSpec(x.shape, lambda i: (0, 0))
    return pl.pallas_call(
        filter_kernel,
        grid=(2 * PIECES,),
        in_specs=[pl.BlockSpec((CHUNK, inputs, samples), lambda i: (i, 0, 0))]
        + halo
        + [whole(taps), whole(gain), whole(weight), whole(table)],
        out_specs=pl.BlockSpec(memory_space=pl.ANY),
        out_shape=jax.ShapeDtypeStruct(shape, jnp.bfloat16),
        scratch_shapes=[
            pltpu.VMEM((CHUNK * inputs, samples), jnp.bfloat16),
            pltpu.VMEM((channels * height, LANES), jnp.float32),
            pltpu.VMEM(shape, jnp.bfloat16),
            pltpu.SemaphoreType.DMA((PIECES, dests)),
            pltpu.SemaphoreType.DMA((PIECES, dests)),
            pltpu.SemaphoreType.DMA((PIECES,)),
        ],
        compiler_params=pltpu.CompilerParams(
            vmem_limit_bytes=56 * 2**20, collective_id=0, has_side_effects=True
        ),
        name="filterbank_send",
    )(turned, turned, turned, turned, taps, gain, weight, table)


def correlate_kernel(slots, *rest, block, frames):
    received, out, stacked, rotated, flipped = rest
    _, sources, _, _, height, _ = received.shape
    half = LANES // 2
    for p in range(PIECES):
        for part in range(2):
            for s in range(0, sources, 2):
                first = received[p, s, 0, part]
                second = received[p, s + 1, 0, part]
                row = part * frames + p * 2 * height
                cols = slice(s * half, s * half + LANES)
                stacked[row : row + height, cols] = jnp.concatenate(
                    [first[:, :half], second[:, :half]], axis=1
                )
                stacked[row + height : row + 2 * height, cols] = jnp.concatenate(
                    [first[:, half:], second[:, half:]], axis=1
                )
    inputs = stacked.shape[1]
    x = stacked[...].astype(jnp.float32)
    total = jnp.sum(x * x, keepdims=True)
    power = total / jnp.float32(inputs * frames * PRESCALE * PRESCALE) + jnp.float32(eps_power)
    scale = lax.rsqrt(power)
    scale = scale * scale * jnp.float32(1.0 / (frames * PRESCALE * PRESCALE))
    flipped[...] = stacked[...].T
    rotated[:frames, :] = -stacked[frames:, :]
    rotated[frames:, :] = stacked[:frames, :]
    blocks = inputs // block
    row_table, col_table = tile_tables(blocks)
    for c in range(blocks):
        cols = slice(c * block, (c + 1) * block)
        for r in range(c + 1):
            tile = [t for t in range(len(row_table)) if row_table[t] == r and col_table[t] == c][0]
            slot = slots[tile]
            left = flipped[r * block : (r + 1) * block, :]
            for part, right in ((0, stacked), (1, rotated)):
                gram = jnp.dot(left, right[:, cols], preferred_element_type=jnp.float32)
                out[0, slot, part] = (gram * scale).astype(jnp.bfloat16)


def correlate(slots, received):
    _, sources, local, _, height, _ = received.shape
    inputs = sources * LANES // 2
    frames = PIECES * height * 2
    tiles = slots.shape[0]
    kernel = functools.partial(correlate_kernel, block=BLK, frames=frames)
    return pl.pallas_call(
        kernel,
        grid_spec=pltpu.PrefetchScalarGridSpec(
            num_scalar_prefetch=1,
            grid=(local,),
            in_specs=[
                pl.BlockSpec(
                    (PIECES, sources, 1, 2, height, LANES), lambda k, *_: (0, 0, k, 0, 0, 0)
                )
            ],
            out_specs=pl.BlockSpec(
                (1, tiles, 2, BLK, BLK), lambda k, *_: (k, 0, 0, 0, 0)
            ),
            scratch_shapes=[
                pltpu.VMEM((2 * frames, inputs), jnp.bfloat16),
                pltpu.VMEM((2 * frames, inputs), jnp.bfloat16),
                pltpu.VMEM((inputs, 2 * frames), jnp.bfloat16),
            ],
        ),
        out_shape=jax.ShapeDtypeStruct((local, tiles, 2, BLK, BLK), jnp.bfloat16),
        compiler_params=pltpu.CompilerParams(vmem_limit_bytes=60 * 2**20),
        cost_estimate=pl.CostEstimate(
            flops=local * tiles * 2 * 2 * BLK * BLK * 2 * frames,
            bytes_accessed=local * (tiles * 2 * BLK * BLK * 2 + inputs * frames * 4),
            transcendentals=0,
        ),
        name="correlate",
    )(slots, received)


def body(voltages, filter_taps, input_gain, input_flags, kept_channels, tile_order):
    local_inputs, padded_frames, samples = voltages.shape
    taps = filter_taps.shape[0]
    frames = padded_frames - taps + 1
    kept = kept_channels.shape[0]
    devices = lax.axis_size("wide")
    fits = (
        local_inputs * 2 == LANES
        and taps == 4
        and frames == PIECES * 2 * CHUNK
        and devices % 2 == 0
        and kept % devices == 0
        and samples % LANES == 0
    )
    if not fits:
        return plain_body(
            voltages, filter_taps, input_gain, input_flags, kept_channels, tile_order
        )
    table = dft_rows(kept_channels, samples)
    turned = jnp.transpose(voltages, (1, 0, 2))
    gain = jnp.broadcast_to(input_gain[:, None], (local_inputs, LANES))
    weight = input_flags.astype(jnp.float32) * jnp.float32(PRESCALE)
    weight = jnp.concatenate([weight, weight])[None, :]
    float_taps = filter_taps.astype(jnp.float32)
    tiles = tile_order.shape[0]
    numbers = jnp.arange(tiles, dtype=jnp.int32)
    slots = jnp.sum(
        jnp.where(tile_order[None, :] == numbers[:, None], numbers[None, :], 0), axis=1
    ).astype(jnp.int32)
    received = filter_and_send(turned, float_taps, gain, weight, table, devices)
    return correlate(slots, received)


def solution(mesh):
    return jax.shard_map(
        body,
        mesh=mesh,
        in_specs=(
            P(("grp", "wide"), None, None),
            P(),
            P(("grp", "wide")),
            P(("grp", "wide")),
            P(),
            P(),
        ),
        out_specs=P(("grp", "wide"), None, None, None, None),
        check_vma=False,
    )
```
